32 devices in a mesh: groups: 2 (over y), expert: 4 (over z), dp: 4 (over x, core).
Axes of the slice: x: 2, y: 2, z: 4, core: 2. Of those that a mesh axis runs over, the one named last changes fastest.
Arguments:
- tokens: bfloat16 [32, 256, 1280], P(('groups', 'expert', 'dp')), parts along dimension 0, may hold values from -8 to 8
- cotangent: bfloat16 [32, 256, 1280], P(('groups', 'expert', 'dp')), parts along dimension 0, may hold values from -6 to 6
- slot_params: bfloat16 [1280, 8], replicated, may hold values from -4 to 4
- inner_weight: bfloat16 [4, 1280, 4096], P('expert', None, 'dp'), may hold values from -0.15625 to 0.15625
- outer_weight: bfloat16 [4, 4096, 1280], P('expert', 'dp'), may hold values from -0.09375 to 0.09375
Outputs:
- grad_tokens: bfloat16 [32, 256, 1280], P(('groups', 'expert', 'dp')), parts along dimension 0
- grad_slot_params: float32 [2560, 8], P('groups'), parts along dimension 0
- grad_inner: bfloat16 [8, 1280, 4096], P(('groups', 'expert'), None, 'dp'), parts along dimension 0
- grad_outer: bfloat16 [8, 4096, 1280], P(('groups', 'expert'), 'dp'), parts along dimension 0
The draws below stay inside these ranges and needn't reach their ends.
There are 2 independent parts, one for each index of `groups`. The reference program is written for one: setup_inputs(seed, part) draws one part's arguments, and reference() takes and returns one part's arrays. A program takes and returns all parts, laid end to end along the dimension named above; an argument that names none is the same for every part. Nothing has to cross between parts.
All inputs are finite; a program needn't handle non-finite values.
Results may differ from the reference program's by a relative error of at most 0.02.
Values may be sent and summed in bfloat16 or wider, within the bound.
A program may use at most 64 MiB of HBM per device.

```python
import jax
import jax.numpy as jnp
from jax import lax

D = 1280
FF = 4096
PATCHES = 256
SLOTS = 2
EXPERTS = 4
IMAGES = 16
FF_DEV = 1024
N_DP = 4


def draw_tokens(key, part):
    key = jax.random.fold_in(key, 11)
    image_count = int(IMAGES)
    patch_count = int(PATCHES)
    width = int(D)
    shape = (image_count, patch_count, width)
    values = jax.random.normal(key, shape, jnp.float32)
    values = jnp.clip(values, -4.0, 4.0)
    return values.astype(jnp.bfloat16)


def draw_slot_params(key, part):
    key = jax.random.fold_in(key, 23)
    width = int(D)
    columns = int(EXPERTS) * int(SLOTS)
    shape = (width, columns)
    base = jnp.clip(jax.random.normal(key, shape, jnp.float32), -4.0, 4.0) * width ** (-0.5)
    values = base
    values = jnp.clip(values, -4.0, 4.0)
    return values.astype(jnp.bfloat16)


def block_scale(rng, dims, shards, low, largest):
    level, own = 1.0, jax.random.fold_in(rng, 6)
    for dim, shards_of in shards:
        heights = jnp.exp(jax.random.uniform(jax.random.fold_in(own, dim), (shards_of,), jnp.float32, low / len(shards), largest / len(shards)))
        level = level * jnp.repeat(heights, dims[dim] // shards_of).reshape([-1 if axis == dim else 1 for axis in range(len(dims))])
    return level


def noise(own_key, extent, scale, bound, split=(), kind=jnp.bfloat16):
    array = scale * jax.random.normal(own_key, extent, jnp.float32)
    if split:
        array = array * block_scale(own_key, extent, split, -0.22, 0.18)
    return jnp.clip(array, -bound, bound).astype(kind)


def setup_inputs(seed: int = 0, part: int = 0) -> dict:
    splits = jax.random.split(jax.random.key(seed), 6)
    part_splits = jax.random.split(jax.random.fold_in(splits[5], part), 6)
    tokens = draw_tokens(jax.random.fold_in(jax.random.fold_in(splits[5], part), 71), part)
    cotangent = noise(part_splits[1], (IMAGES, PATCHES, D), 1.0, 6.0, ((0, 16),))
    slot_params = draw_slot_params(jax.random.fold_in(splits[5], 71), part)
    inner_weight = noise(splits[3], (EXPERTS, D, FF), D ** -0.5, 0.15625, ((0, 4), (2, 4)))
    outer_weight = noise(splits[4], (EXPERTS, FF, D), FF ** -0.5, 0.09375, ((0, 4), (1, 4)))
    return dict(tokens=tokens, cotangent=cotangent, slot_params=slot_params, inner_weight=inner_weight, outer_weight=outer_weight)


def gelu_tanh(values):
    return jax.nn.gelu(values, approximate=True)

def block_partials(left, right):
    count = left.shape[0]
    left_blocks = left.reshape(count, SLOTS, N_DP, FF_DEV).astype(jnp.float32)
    right_blocks = right.reshape(N_DP, FF_DEV, D).astype(jnp.float32)
    partial_value = jnp.einsum('nsbf,bfd->nsbd', left_blocks, right_blocks)
    rounded = lax.optimization_barrier(partial_value.astype(jnp.bfloat16))
    return lax.optimization_barrier(jnp.sum(rounded.astype(jnp.float32), axis=2))

def by_expert(values):
    return values.reshape(IMAGES, EXPERTS, SLOTS, D).transpose(1, 0, 2, 3)

def by_image(values):
    return values.transpose(1, 0, 2, 3).reshape(IMAGES, EXPERTS * SLOTS, D)

def reference(tokens, cotangent, slot_params, inner_weight, outer_weight):
    tok_f = tokens.astype(jnp.float32)
    params_f = slot_params.astype(jnp.float32)
    logits = jnp.einsum('itd,dc->ict', tok_f, params_f)
    dispatch_exact = jax.nn.softmax(logits, axis=2)
    combine_exact = jax.nn.softmax(logits, axis=1)
    dispatch = dispatch_exact.astype(jnp.bfloat16)
    combine = combine_exact.astype(jnp.bfloat16)
    slot_in = jnp.einsum('ict,itd->icd', dispatch.astype(jnp.float32), tok_f).astype(jnp.bfloat16)
    grouped = by_expert(slot_in)

    def forward_one(operands):
        rows, first, second = operands
        preact = jnp.einsum('nsd,df->nsf', rows.astype(jnp.float32), first.astype(jnp.float32))
        hidden = gelu_tanh(preact).astype(jnp.bfloat16)
        return block_partials(hidden, second).astype(jnp.bfloat16)
    slot_out = by_image(lax.map(forward_one, (grouped, inner_weight, outer_weight)))
    cot_f = cotangent.astype(jnp.float32)
    g_slot_out = jnp.einsum('ict,itd->icd', combine.astype(jnp.float32), cot_f).astype(jnp.bfloat16)
    g_combine = jnp.einsum('itd,icd->ict', cot_f, slot_out.astype(jnp.float32))
    g_logit_combine = combine_exact * (g_combine - lax.optimization_barrier(jnp.sum(combine_exact * g_combine, axis=1, keepdims=True)))

    def backward_one(operands):
        rows, grad_rows, first, second = operands
        preact = jnp.einsum('nsd,df->nsf', rows.astype(jnp.float32), first.astype(jnp.float32))
        hidden = gelu_tanh(preact).astype(jnp.bfloat16)
        outer_grad = jnp.einsum('nsf,nsd->fd', hidden.astype(jnp.float32), grad_rows.astype(jnp.float32)).astype(jnp.bfloat16)
        g_hidden = jnp.einsum('nsd,fd->nsf', grad_rows.astype(jnp.float32), second.astype(jnp.float32))
        unused, pull = jax.vjp(gelu_tanh, preact)
        g_preact = pull(g_hidden)[0].astype(jnp.bfloat16)
        inner_grad = jnp.einsum('nsd,nsf->df', rows.astype(jnp.float32), g_preact.astype(jnp.float32)).astype(jnp.bfloat16)
        g_rows = block_partials(g_preact, first.T).astype(jnp.bfloat16)
        return (g_rows, inner_grad, outer_grad)
    g_grouped, grad_inner, grad_outer = lax.map(backward_one, (grouped, by_expert(g_slot_out), inner_weight, outer_weight))
    g_slot_in = by_image(g_grouped)
    g_dispatch = jnp.einsum('itd,icd->ict', tok_f, g_slot_in.astype(jnp.float32))
    g_logit_dispatch = dispatch_exact * (g_dispatch - lax.optimization_barrier(jnp.sum(dispatch_exact * g_dispatch, axis=2, keepdims=True)))
    g_logits = (g_logit_combine + g_logit_dispatch).astype(jnp.bfloat16)
    g_logits_f = g_logits.astype(jnp.float32)
    grad_tokens = (jnp.einsum('ict,icd->itd', dispatch.astype(jnp.float32), g_slot_in.astype(jnp.float32)) + jnp.einsum('ict,dc->itd', g_logits_f, params_f)).astype(jnp.bfloat16)
    grad_slot_params = jnp.einsum('itd,ict->dc', tok_f, g_logits_f)
    return (grad_tokens, grad_slot_params, grad_inner, grad_outer)
```

```python
import functools

import jax
import jax.numpy as jnp
from jax import lax
from jax.experimental import pallas as pl
from jax.experimental.pallas import tpu as pltpu
from jax.sharding import PartitionSpec as P

F32, BF16 = jnp.float32, jnp.bfloat16
MESH = pl.DeviceIdType.MESH
ROWS, PIECES = 4, 4
MSG = ROWS * PIECES
CHUNK = 16


def dot(a, b, contract, out=F32):
    return lax.dot_general(a, b, ((contract[:1], contract[1:]), ((), ())), preferred_element_type=out)


def pieces_of(width):
    step = -(-width // (PIECES * 128)) * 128
    return step, [(q * step, min(width, (q + 1) * step)) for q in range(PIECES)]


def select(messages, q):
    shape = (messages * ROWS, messages * MSG)
    row = lax.broadcasted_iota(jnp.int32, shape, 0)
    line = lax.broadcasted_iota(jnp.int32, shape, 1)
    half = (row >= messages * 2).astype(jnp.int32)
    inner = row - half * (messages * 2)
    target = (inner >> 1) * MSG + q * ROWS + half * 2 + (inner & 1)
    return (line == target).astype(BF16)


def pack(rows, messages):
    width = rows.shape[1]
    step, spans = pieces_of(width)
    total = None
    for q, (low, high) in enumerate(spans):
        piece = rows[:, low:high]
        if high - low < step:
            piece = jnp.concatenate([piece, jnp.zeros((rows.shape[0], step - high + low), BF16)], axis=1)
        part = dot(select(messages, q), piece, (0, 0))
        total = part if total is None else total + part
    return total.astype(BF16)


def kernel(
    experts, dp_size, tokens_ref, cot_ref, params_ref, inner_hbm, outer_hbm,
    gtok_ref, gparams_ref, x_ref, g_ref, hidden_ref, gpre_ref,
    inner_ref, outer_ref, send1, recv1, send2, recv2, part_a, part_b,
    load_sem, send_sem, recv_sem,
):
    peers = experts * dp_size
    expert = lax.axis_index("expert")
    dp = lax.axis_index("dp")
    me = expert * dp_size + dp
    width = tokens_ref.shape[1]
    step, spans = pieces_of(width)
    columns = params_ref.shape[0]
    half = width // 2

    load_inner = pltpu.make_async_copy(inner_hbm, inner_ref, load_sem.at[0])
    load_outer = pltpu.make_async_copy(outer_hbm, outer_ref, load_sem.at[1])
    load_inner.start()
    load_outer.start()

    def device(peer):
        return {"expert": lax.div(peer, dp_size), "dp": lax.rem(peer, dp_size)}

    barrier = pltpu.get_barrier_semaphore()

    @pl.loop(1, peers)
    def _(offset):
        pl.semaphore_signal(
            barrier, inc=1, device_id=device(lax.rem(me + offset, peers)), device_id_type=MESH
        )

    tokens = tokens_ref[...]
    logits = dot(params_ref[...], tokens, (1, 1))
    e_t = jnp.exp(logits - jnp.max(logits, axis=1, keepdims=True))
    dispatch_exact = e_t / jnp.sum(e_t, axis=1, keepdims=True)
    e_c = jnp.exp(logits - jnp.max(logits, axis=0, keepdims=True))
    combine_exact = e_c / jnp.sum(e_c, axis=0, keepdims=True)
    dispatch = dispatch_exact.astype(BF16)
    slot_in = dot(dispatch, tokens, (1, 0))
    g_slot_out = dot(combine_exact.astype(BF16), cot_ref[...], (1, 0))
    both = jnp.concatenate([slot_in, g_slot_out], axis=0).astype(BF16)
    send1[...] = pack(both, experts).reshape(experts, MSG, step)
    recv1[pl.ds(me, 1)] = send1[pl.ds(expert, 1)]

    pl.semaphore_wait(barrier, peers - 1)

    def exchange(index, source, target):
        @pl.loop(1, peers)
        def _(offset):
            peer = lax.rem(me + offset, peers)
            pltpu.make_async_remote_copy(
                src_ref=source(peer), dst_ref=target.at[me], send_sem=send_sem.at[index],
                recv_sem=recv_sem.at[index], device_id=device(peer), device_id_type=MESH,
            ).start()

    def wait(index, target, count):
        whole = target.at[pl.ds(0, count)]
        copy = pltpu.make_async_remote_copy(
            src_ref=whole, dst_ref=whole, send_sem=send_sem.at[index],
            recv_sem=recv_sem.at[index], device_id={"expert": expert, "dp": dp}, device_id_type=MESH,
        )
        copy.wait_recv()
        copy.wait_send()

    exchange(0, lambda peer: send1.at[lax.div(peer, dp_size)], recv1)
    wait(0, recv1, peers - 1)

    chunk = min(CHUNK, peers)
    lines = chunk * 2

    @pl.loop(0, peers // chunk)
    def _(index):
        block = recv1[pl.ds(index * chunk, chunk)].reshape(chunk * MSG, step)
        at = pl.ds(pl.multiple_of(index * lines, lines), lines)
        for q, (low, high) in enumerate(spans):
            piece = dot(select(chunk, q), block[:, : high - low], (1, 0)).astype(BF16)
            x_ref[at, low:high] = piece[:lines]
            g_ref[at, low:high] = piece[lines:]

    load_inner.wait()
    load_outer.wait()
    rows, g_rows = x_ref[...], g_ref[...]
    pre = dot(rows, inner_ref[...], (1, 0))
    g_hidden = dot(g_rows, outer_ref[...], (1, 1))
    scale = 0.7978845608028654
    tanh = jnp.tanh(scale * (pre + 0.044715 * (pre * pre * pre)))
    gate = 0.5 * (1.0 + tanh)
    hidden = (pre * gate).astype(BF16)
    slope = gate + (0.5 * pre) * (1.0 - tanh * tanh) * (scale * (1.0 + 0.134145 * (pre * pre)))
    g_pre = (g_hidden * slope).astype(BF16)
    hidden_ref[...] = hidden
    gpre_ref[...] = g_pre
    out_part = dot(hidden, outer_ref[...], (1, 0)).astype(BF16)
    g_part = dot(g_pre, inner_ref[...], (1, 1)).astype(BF16)
    for index in range(peers // chunk):
        at = slice(index * lines, (index + 1) * lines)
        both = jnp.concatenate([out_part[at], g_part[at]], axis=0)
        send2[index * chunk : (index + 1) * chunk] = pack(both, chunk).reshape(chunk, MSG, step)
    recv2[pl.ds(me, 1)] = send2[pl.ds(me, 1)]
    exchange(1, lambda peer: send2.at[peer], recv2)
    wait(1, recv2, peers - 1)

    block = recv2[...].reshape(peers * MSG, step)
    shape = (2 * columns, peers * MSG)
    row = lax.broadcasted_iota(jnp.int32, shape, 0)
    line = lax.broadcasted_iota(jnp.int32, shape, 1)
    second = (row >= columns).astype(jnp.int32)
    column = row - second * columns
    per_expert = dp_size * MSG
    wanted = second * 2 + (column & 1)
    base = (column >> 1) * per_expert
    inside = (line >= base) & (line < base + per_expert)
    sums = []
    for q, (low, high) in enumerate(spans):
        take = (inside & ((line & (MSG - 1)) == wanted + q * ROWS)).astype(BF16)
        sums.append(dot(take, block[:, : high - low], (1, 0)))
    total = jnp.concatenate(sums, axis=1)
    slot_out = total[:columns].astype(BF16)
    g_slot_in = total[columns:].astype(BF16)

    g_combine = dot(slot_out, cot_ref[...], (1, 1))
    g_logit = combine_exact * (
        g_combine - jnp.sum(combine_exact * g_combine, axis=0, keepdims=True)
    )
    g_dispatch = dot(g_slot_in, tokens, (1, 1))
    g_logit = g_logit + dispatch_exact * (
        g_dispatch - jnp.sum(dispatch_exact * g_dispatch, axis=1, keepdims=True)
    )
    g_logits = g_logit.astype(BF16)
    local = dot(g_logits, tokens, (1, 0))

    def fold(values):
        return jnp.concatenate([values[:, :half], values[:, half:]], axis=0).astype(BF16)

    def spread(index, target, own, axis, size):
        @pl.loop(1, size)
        def _(offset):
            other = lax.rem(own + offset, size)
            where = {"expert": expert, "dp": dp}
            where[axis] = other
            pltpu.make_async_remote_copy(
                src_ref=target.at[own], dst_ref=target.at[own], send_sem=send_sem.at[index],
                recv_sem=recv_sem.at[index], device_id=where, device_id_type=MESH,
            ).start()

    def add(target, size):
        folded = target[0].astype(F32)
        for index in range(1, size):
            folded = folded + target[index].astype(F32)
        return folded

    part_a[pl.ds(dp, 1)] = fold(local)[None]
    spread(2, part_a, dp, "dp", dp_size)
    left = jnp.concatenate([dispatch_exact, g_logits.astype(F32)], axis=0).astype(BF16)
    right = jnp.concatenate([g_slot_in.astype(F32), params_ref[...].astype(F32)], axis=0).astype(BF16)
    gtok_ref[...] = dot(left, right, (0, 0)).astype(BF16)
    wait(2, part_a, dp_size - 1)
    part_b[pl.ds(expert, 1)] = add(part_a, dp_size).astype(BF16)[None]
    spread(3, part_b, expert, "expert", experts)
    wait(3, part_b, experts - 1)
    folded = add(part_b, experts)
    gparams_ref[:, :half] = folded[:columns]
    gparams_ref[:, half:] = folded[columns:]


def local(tokens, cotangent, slot_params, inner_weight, outer_weight):
    width = tokens.shape[2]
    patches = tokens.shape[1]
    columns = slot_params.shape[1]
    experts = lax.axis_size("expert")
    dp_size = lax.axis_size("dp")
    peers = experts * dp_size
    units = inner_weight.shape[2]
    rows = peers * 2
    step, _ = pieces_of(width)
    vmem = pl.BlockSpec(memory_space=pltpu.VMEM)
    hbm = pl.BlockSpec(memory_space=pl.ANY)
    shape = jax.ShapeDtypeStruct
    g_tokens, g_params, x, g, hidden, g_pre = pl.pallas_call(
        functools.partial(kernel, experts, dp_size),
        out_shape=[
            shape((patches, width), BF16),
            shape((columns, width), F32),
            shape((rows, width), BF16),
            shape((rows, width), BF16),
            shape((rows, units), BF16),
            shape((rows, units), BF16),
        ],
        in_specs=[vmem, vmem, vmem, hbm, hbm],
        out_specs=[vmem] * 6,
        scratch_shapes=[
            pltpu.VMEM((width, units), BF16),
            pltpu.VMEM((units, width), BF16),
            pltpu.VMEM((experts, MSG, step), BF16),
            pltpu.VMEM((peers, MSG, step), BF16),
            pltpu.VMEM((peers, MSG, step), BF16),
            pltpu.VMEM((peers, MSG, step), BF16),
            pltpu.VMEM((dp_size, 2 * columns, width // 2), BF16),
            pltpu.VMEM((experts, 2 * columns, width // 2), BF16),
            pltpu.SemaphoreType.DMA((2,)),
            pltpu.SemaphoreType.DMA((4,)),
            pltpu.SemaphoreType.DMA((4,)),
        ],
        compiler_params=pltpu.CompilerParams(
            collective_id=0, has_side_effects=True, vmem_limit_bytes=48 * 1024 * 1024
        ),
    )(tokens[0], cotangent[0], slot_params.T, inner_weight[0], outer_weight[0])
    grad_inner = dot(x, g_pre, (0, 0)).astype(BF16)
    grad_outer = dot(hidden, g, (0, 0)).astype(BF16)
    return g_tokens[None], g_params.T, grad_inner[None], grad_outer[None]


def solution(mesh):
    return jax.shard_map(
        local,
        mesh=mesh,
        in_specs=(
            P(("groups", "expert", "dp"), None, None),
            P(("groups", "expert", "dp"), None, None),
            P(),
            P("expert", None, "dp"),
            P("expert", "dp", None),
        ),
        out_specs=(
            P(("groups", "expert", "dp"), None, None),
            P("groups", None),
            P(("groups", "expert"), None, "dp"),
            P(("groups", "expert"), "dp", None),
        ),
        check_vma=False,
    )
```

```python
import functools

import jax
import jax.numpy as jnp
from jax import lax
from jax.experimental import pallas as pl
from jax.experimental.pallas import tpu as pltpu
from jax.sharding import PartitionSpec as P

F32, BF16 = jnp.float32, jnp.bfloat16
MESH = pl.DeviceIdType.MESH
ROWS, PIECES = 4, 4
MSG = ROWS * PIECES
CHUNK = 16
VMEM_BYTES = 60 * 1024 * 1024


def dot(a, b, contract, out=F32):
    return lax.dot_general(a, b, ((contract[:1], contract[1:]), ((), ())), preferred_element_type=out)


def pieces_of(width):
    step = -(-width // (PIECES * 128)) * 128
    return step, [(q * step, min(width, (q + 1) * step)) for q in range(PIECES)]


def select(messages, q):
    shape = (messages * ROWS, messages * MSG)
    row = lax.broadcasted_iota(jnp.int32, shape, 0)
    line = lax.broadcasted_iota(jnp.int32, shape, 1)
    half = (row >= messages * 2).astype(jnp.int32)
    inner = row - half * (messages * 2)
    target = (inner >> 1) * MSG + q * ROWS + half * 2 + (inner & 1)
    return (line == target).astype(BF16)


def pack(rows, messages):
    width = rows.shape[1]
    step, spans = pieces_of(width)
    total = None
    for q, (low, high) in enumerate(spans):
        piece = rows[:, low:high]
        if high - low < step:
            piece = jnp.concatenate([piece, jnp.zeros((rows.shape[0], step - high + low), BF16)], axis=1)
        part = dot(select(messages, q), piece, (0, 0))
        total = part if total is None else total + part
    return total.astype(BF16)


def kernel(
    experts, dp_size, tokens_hbm, cot_hbm, params_hbm, inner_hbm, outer_hbm,
    x_hbm, g_hbm, hidden_hbm, gpre_hbm, left_hbm, right_hbm, gparams_hbm,
    x_ref, g_ref, hidden_ref, gpre_ref, left_ref, right_ref, gparams_ref,
    tokens_ref, cot_ref, params_ref, inner_ref, outer_ref, send1, recv1, send2, recv2, part_a, part_b,
    load_sem, store_sem, send_sem, recv_sem,
):
    peers = experts * dp_size
    expert = lax.axis_index("expert")
    dp = lax.axis_index("dp")
    me = expert * dp_size + dp
    width = tokens_ref.shape[1]
    step, spans = pieces_of(width)
    columns = params_ref.shape[0]
    half = width // 2

    pairs = (
        (params_hbm, params_ref), (tokens_hbm, tokens_ref), (cot_hbm, cot_ref),
        (inner_hbm, inner_ref), (outer_hbm, outer_ref),
    )
    loads = [pltpu.make_async_copy(a, b, load_sem.at[i]) for i, (a, b) in enumerate(pairs)]
    pairs = (
        (x_ref, x_hbm), (g_ref, g_hbm), (hidden_ref, hidden_hbm), (gpre_ref, gpre_hbm),
        (left_ref, left_hbm), (right_ref, right_hbm), (gparams_ref, gparams_hbm),
    )
    stores = [pltpu.make_async_copy(a, b, store_sem.at[i]) for i, (a, b) in enumerate(pairs)]
    for load in loads:
        load.start()

    def device(peer):
        return {"expert": lax.div(peer, dp_size), "dp": lax.rem(peer, dp_size)}

    barrier = pltpu.get_barrier_semaphore()

    @pl.loop(1, peers)
    def _(offset):
        pl.semaphore_signal(
            barrier, inc=1, device_id=device(lax.rem(me + offset, peers)), device_id_type=MESH
        )

    loads[0].wait()
    loads[1].wait()
    tokens = tokens_ref[...]
    logits = dot(params_ref[...], tokens, (1, 1))
    e_t = jnp.exp(logits - jnp.max(logits, axis=1, keepdims=True))
    dispatch_exact = e_t / jnp.sum(e_t, axis=1, keepdims=True)
    e_c = jnp.exp(logits - jnp.max(logits, axis=0, keepdims=True))
    combine_exact = e_c / jnp.sum(e_c, axis=0, keepdims=True)
    dispatch = dispatch_exact.astype(BF16)
    slot_in = dot(dispatch, tokens, (1, 0))
    loads[2].wait()
    g_slot_out = dot(combine_exact.astype(BF16), cot_ref[...], (1, 0))
    both = jnp.concatenate([slot_in, g_slot_out], axis=0).astype(BF16)
    send1[...] = pack(both, experts).reshape(experts, MSG, step)
    recv1[pl.ds(me, 1)] = send1[pl.ds(expert, 1)]

    pl.semaphore_wait(barrier, peers - 1)

    def exchange(index, source, target):
        @pl.loop(1, peers)
        def _(offset):
            peer = lax.rem(me + offset, peers)
            pltpu.make_async_remote_copy(
                src_ref=source(peer), dst_ref=target.at[me], send_sem=send_sem.at[index],
                recv_sem=recv_sem.at[index], device_id=device(peer), device_id_type=MESH,
            ).start()

    def wait(index, target, count):
        whole = target.at[pl.ds(0, count)]
        copy = pltpu.make_async_remote_copy(
            src_ref=whole, dst_ref=whole, send_sem=send_sem.at[index],
            recv_sem=recv_sem.at[index], device_id={"expert": expert, "dp": dp}, device_id_type=MESH,
        )
        copy.wait_recv()
        copy.wait_send()

    exchange(0, lambda peer: send1.at[lax.div(peer, dp_size)], recv1)
    wait(0, recv1, peers - 1)

    chunk = min(CHUNK, peers)
    lines = chunk * 2

    @pl.loop(0, peers // chunk)
    def _(index):
        block = recv1[pl.ds(index * chunk, chunk)].reshape(chunk * MSG, step)
        at = pl.ds(pl.multiple_of(index * lines, lines), lines)
        for q, (low, high) in enumerate(spans):
            piece = dot(select(chunk, q), block[:, : high - low], (1, 0)).astype(BF16)
            x_ref[at, low:high] = piece[:lines]
            g_ref[at, low:high] = piece[lines:]

    loads[3].wait()
    loads[4].wait()
    stores[0].start()
    stores[1].start()
    rows, g_rows = x_ref[...], g_ref[...]
    pre = dot(rows, inner_ref[...], (1, 0))
    g_hidden = dot(g_rows, outer_ref[...], (1, 1))
    scale = 0.7978845608028654
    tanh = jnp.tanh(scale * (pre + 0.044715 * (pre * pre * pre)))
    gate = 0.5 * (1.0 + tanh)
    hidden = (pre * gate).astype(BF16)
    slope = gate + (0.5 * pre) * (1.0 - tanh * tanh) * (scale * (1.0 + 0.134145 * (pre * pre)))
    g_pre = (g_hidden * slope).astype(BF16)
    hidden_ref[...] = hidden
    gpre_ref[...] = g_pre
    stores[2].start()
    stores[3].start()
    out_part = dot(hidden, outer_ref[...], (1, 0)).astype(BF16)
    g_part = dot(g_pre, inner_ref[...], (1, 1)).astype(BF16)
    for index in range(peers // chunk):
        at = slice(index * lines, (index + 1) * lines)
        both = jnp.concatenate([out_part[at], g_part[at]], axis=0)
        send2[index * chunk : (index + 1) * chunk] = pack(both, chunk).reshape(chunk, MSG, step)
    recv2[pl.ds(me, 1)] = send2[pl.ds(me, 1)]
    exchange(1, lambda peer: send2.at[peer], recv2)
    wait(1, recv2, peers - 1)

    block = recv2[...].reshape(peers * MSG, step)
    shape = (2 * columns, peers * MSG)
    row = lax.broadcasted_iota(jnp.int32, shape, 0)
    line = lax.broadcasted_iota(jnp.int32, shape, 1)
    second = (row >= columns).astype(jnp.int32)
    column = row - second * columns
    per_expert = dp_size * MSG
    wanted = second * 2 + (column & 1)
    base = (column >> 1) * per_expert
    inside = (line >= base) & (line < base + per_expert)
    sums = []
    for q, (low, high) in enumerate(spans):
        take = (inside & ((line & (MSG - 1)) == wanted + q * ROWS)).astype(BF16)
        sums.append(dot(take, block[:, : high - low], (1, 0)))
    total = jnp.concatenate(sums, axis=1)
    slot_out = total[:columns].astype(BF16)
    g_slot_in = total[columns:].astype(BF16)

    g_combine = dot(slot_out, cot_ref[...], (1, 1))
    g_logit = combine_exact * (
        g_combine - jnp.sum(combine_exact * g_combine, axis=0, keepdims=True)
    )
    g_dispatch = dot(g_slot_in, tokens, (1, 1))
    g_logit = g_logit + dispatch_exact * (
        g_dispatch - jnp.sum(dispatch_exact * g_dispatch, axis=1, keepdims=True)
    )
    g_logits = g_logit.astype(BF16)
    local = dot(g_logits, tokens, (1, 0))

    def fold(values):
        return jnp.concatenate([values[:, :half], values[:, half:]], axis=0).astype(BF16)

    def spread(index, target, own, axis, size):
        @pl.loop(1, size)
        def _(offset):
            other = lax.rem(own + offset, size)
            where = {"expert": expert, "dp": dp}
            where[axis] = other
            pltpu.make_async_remote_copy(
                src_ref=target.at[own], dst_ref=target.at[own], send_sem=send_sem.at[index],
                recv_sem=recv_sem.at[index], device_id=where, device_id_type=MESH,
            ).start()

    def add(target, size):
        folded = target[0].astype(F32)
        for index in range(1, size):
            folded = folded + target[index].astype(F32)
        return folded

    part_a[pl.ds(dp, 1)] = fold(local)[None]
    spread(2, part_a, dp, "dp", dp_size)
    left_ref[...] = jnp.concatenate([dispatch_exact, g_logits.astype(F32)], axis=0).astype(BF16)
    right_ref[:columns] = g_slot_in
    right_ref[columns:] = params_ref[...]
    stores[4].start()
    stores[5].start()
    wait(2, part_a, dp_size - 1)
    part_b[pl.ds(expert, 1)] = add(part_a, dp_size).astype(BF16)[None]
    spread(3, part_b, expert, "expert", experts)
    wait(3, part_b, experts - 1)
    folded = add(part_b, experts)
    gparams_ref[:, :half] = folded[:columns]
    gparams_ref[:, half:] = folded[columns:]
    stores[6].start()
    for store in stores:
        store.wait()


def weight_kernel(
    x_hbm, g_hbm, hidden_hbm, gpre_hbm, left_hbm, right_hbm, gparams_hbm,
    gtok_hbm, gout_hbm, ginner_hbm, gouter_hbm,
    x_ref, g_ref, hidden_ref, gpre_ref, left_ref, right_ref, gparams_ref,
    gtok_ref, ginner_ref, gouter_ref, load_sem, store_sem,
):
    pairs = (
        (x_hbm, x_ref), (gpre_hbm, gpre_ref), (hidden_hbm, hidden_ref), (g_hbm, g_ref),
        (left_hbm, left_ref), (right_hbm, right_ref), (gparams_hbm, gparams_ref),
    )
    loads = [pltpu.make_async_copy(a, b, load_sem.at[i]) for i, (a, b) in enumerate(pairs)]
    for load in loads:
        load.start()
    stores = []

    def product(left, right, out_ref, out_hbm):
        for low in range(0, out_ref.shape[0], 256):
            at = slice(low, min(low + 256, out_ref.shape[0]))
            out_ref[at] = dot(left[:, at], right[...], (0, 0)).astype(BF16)
            stores.append(pltpu.make_async_copy(
                out_ref.at[at], out_hbm.at[at], store_sem.at[len(stores)]
            ))
            stores[-1].start()

    loads[0].wait()
    loads[1].wait()
    product(x_ref, gpre_ref, ginner_ref, ginner_hbm)
    loads[2].wait()
    loads[3].wait()
    product(hidden_ref, g_ref, gouter_ref, gouter_hbm)
    loads[4].wait()
    loads[5].wait()
    product(left_ref, right_ref, gtok_ref, gtok_hbm)
    loads[6].wait()
    stores.append(pltpu.make_async_copy(gparams_ref, gout_hbm, store_sem.at[len(stores)]))
    stores[-1].start()
    for store in stores:
        store.wait()


def local(tokens, cotangent, slot_params, inner_weight, outer_weight):
    width = tokens.shape[2]
    patches = tokens.shape[1]
    columns = slot_params.shape[1]
    experts = lax.axis_size("expert")
    dp_size = lax.axis_size("dp")
    peers = experts * dp_size
    units = inner_weight.shape[2]
    rows = peers * 2
    step, _ = pieces_of(width)
    hbm = pl.BlockSpec(memory_space=pl.ANY)
    shape = jax.ShapeDtypeStruct
    small = (
        shape((rows, width), BF16),
        shape((rows, width), BF16),
        shape((rows, units), BF16),
        shape((rows, units), BF16),
        shape((2 * columns, patches), BF16),
        shape((2 * columns, width), BF16),
        shape((columns, width), F32),
    )
    held = [pltpu.VMEM(s.shape, s.dtype) for s in small]
    small = pl.pallas_call(
        functools.partial(kernel, experts, dp_size),
        out_shape=small,
        in_specs=[hbm] * 5,
        out_specs=[hbm] * 7,
        scratch_shapes=held + [
            pltpu.VMEM((patches, width), BF16),
            pltpu.VMEM((patches, width), BF16),
            pltpu.VMEM((columns, width), BF16),
            pltpu.VMEM((width, units), BF16),
            pltpu.VMEM((units, width), BF16),
            pltpu.VMEM((experts, MSG, step), BF16),
            pltpu.VMEM((peers, MSG, step), BF16),
            pltpu.VMEM((peers, MSG, step), BF16),
            pltpu.VMEM((peers, MSG, step), BF16),
            pltpu.VMEM((dp_size, 2 * columns, width // 2), BF16),
            pltpu.VMEM((experts, 2 * columns, width // 2), BF16),
            pltpu.SemaphoreType.DMA((5,)),
            pltpu.SemaphoreType.DMA((7,)),
            pltpu.SemaphoreType.DMA((4,)),
            pltpu.SemaphoreType.DMA((4,)),
        ],
        compiler_params=pltpu.CompilerParams(
            collective_id=0, has_side_effects=True, vmem_limit_bytes=VMEM_BYTES
        ),
    )(tokens[0], cotangent[0], slot_params.T, inner_weight[0], outer_weight[0])
    results = (
        shape((patches, width), BF16),
        shape((columns, width), F32),
        shape((width, units), BF16),
        shape((units, width), BF16),
    )
    store_count = 1 + sum(-(-n // 256) for n in (patches, width, units))
    g_tokens, g_params, grad_inner, grad_outer = pl.pallas_call(
        weight_kernel,
        out_shape=results,
        in_specs=[hbm] * 7,
        out_specs=[hbm] * 4,
        scratch_shapes=held + [
            pltpu.VMEM((patches, width), BF16),
            pltpu.VMEM((width, units), BF16),
            pltpu.VMEM((units, width), BF16),
            pltpu.SemaphoreType.DMA((7,)),
            pltpu.SemaphoreType.DMA((store_count,)),
        ],
        compiler_params=pltpu.CompilerParams(vmem_limit_bytes=VMEM_BYTES),
    )(*small)
    return g_tokens[None], g_params.T, grad_inner[None], grad_outer[None]


def solution(mesh):
    return jax.shard_map(
        local,
        mesh=mesh,
        in_specs=(
            P(("groups", "expert", "dp"), None, None),
            P(("groups", "expert", "dp"), None, None),
            P(),
            P("expert", None, "dp"),
            P("expert", "dp", None),
        ),
        out_specs=(
            P(("groups", "expert", "dp"), None, None),
            P("groups", None),
            P(("groups", "expert"), None, "dp"),
            P(("groups", "expert"), "dp", None),
        ),
        check_vma=False,
    )
```

```python
import functools

import jax
import jax.numpy as jnp
from jax import lax
from jax.experimental import pallas as pl
from jax.experimental.pallas import tpu as pltpu
from jax.sharding import PartitionSpec as P

F32, BF16 = jnp.float32, jnp.bfloat16
MESH = pl.DeviceIdType.MESH
ROWS, PIECES = 4, 4
MSG = ROWS * PIECES
CHUNK = 16
VMEM_BYTES = 54500 * 1024


def dot(a, b, contract, out=F32):
    return lax.dot_general(a, b, ((contract[:1], contract[1:]), ((), ())), preferred_element_type=out)


def pieces_of(width):
    step = -(-width // (PIECES * 128)) * 128
    return step, [(q * step, min(width, (q + 1) * step)) for q in range(PIECES)]


def select(messages):
    shape = (messages * ROWS, messages * MSG)
    row = lax.broadcasted_iota(jnp.int32, shape, 0)
    line = lax.broadcasted_iota(jnp.int32, shape, 1)
    half = (row >= messages * 2).astype(jnp.int32)
    inner = row - half * (messages * 2)
    shift = line - ((inner >> 1) * MSG + half * 2 + (inner & 1))
    return [(shift == q * ROWS).astype(BF16) for q in range(PIECES)]


def pack(rows, messages, chosen):
    width = rows.shape[1]
    step, spans = pieces_of(width)
    total = None
    for q, (low, high) in enumerate(spans):
        piece = rows[:, low:high]
        if high - low < step:
            piece = jnp.concatenate([piece, jnp.zeros((rows.shape[0], step - high + low), BF16)], axis=1)
        part = dot(chosen[q], piece, (0, 0))
        total = part if total is None else total + part
    return total.astype(BF16)


def kernel(
    experts, dp_size, tokens_hbm, cot_hbm, params_hbm, inner_hbm, outer_hbm,
    x_ref, g_ref, hidden_ref, gpre_ref, left_ref, right_ref, gparams_ref,
    tokens_ref, cot_ref, params_ref, inner_ref, outer_ref, send1, recv1, send2, recv2, part_a, part_b,
    load_sem, send_sem, recv_sem,
):
    peers = experts * dp_size
    expert = lax.axis_index("expert")
    dp = lax.axis_index("dp")
    me = expert * dp_size + dp
    width = tokens_ref.shape[1]
    step, spans = pieces_of(width)
    columns = params_ref.shape[0]
    half = width // 2

    pairs = (
        (params_hbm, params_ref), (tokens_hbm, tokens_ref), (cot_hbm, cot_ref),
        (inner_hbm, inner_ref), (outer_hbm, outer_ref),
    )
    loads = [pltpu.make_async_copy(a, b, load_sem.at[i]) for i, (a, b) in enumerate(pairs)]
    for load in loads:
        load.start()

    def shifted(own, offset, size):
        moved = own + offset
        return jnp.where(moved >= size, moved - size, moved)

    def every_peer(body):
        if peers <= CHUNK:
            for across in range(experts):
                for along in range(dp_size):
                    if across or along:
                        body(shifted(expert, across, experts), shifted(dp, along, dp_size))
        else:
            @pl.loop(1, peers)
            def _(offset):
                body(
                    shifted(expert, lax.div(offset, dp_size), experts),
                    shifted(dp, lax.rem(offset, dp_size), dp_size),
                )

    barrier = pltpu.get_barrier_semaphore()

    def greet(to_expert, to_dp):
        pl.semaphore_signal(
            barrier, inc=1, device_id={"expert": to_expert, "dp": to_dp}, device_id_type=MESH
        )

    every_peer(greet)
    chunk = min(CHUNK, peers)
    lines = chunk * 2
    of_experts, of_chunk = select(experts), select(chunk)

    loads[0].wait()
    loads[1].wait()
    tokens = tokens_ref[...]
    logits = dot(params_ref[...], tokens, (1, 1))
    e_t = jnp.exp(logits - jnp.max(logits, axis=1, keepdims=True))
    dispatch_exact = e_t / jnp.sum(e_t, axis=1, keepdims=True)
    e_c = jnp.exp(logits - jnp.max(logits, axis=0, keepdims=True))
    combine_exact = e_c / jnp.sum(e_c, axis=0, keepdims=True)
    dispatch = dispatch_exact.astype(BF16)
    slot_in = dot(dispatch, tokens, (1, 0))
    loads[2].wait()
    g_slot_out = dot(combine_exact.astype(BF16), cot_ref[...], (1, 0))
    both = jnp.concatenate([slot_in, g_slot_out], axis=0).astype(BF16)
    send1[...] = pack(both, experts, of_experts).reshape(experts, MSG, step)
    recv1[pl.ds(me, 1)] = send1[pl.ds(expert, 1)]

    pl.semaphore_wait(barrier, peers - 1)

    def exchange(index, source, target):
        def send(to_expert, to_dp):
            pltpu.make_async_remote_copy(
                src_ref=source(to_expert, to_dp), dst_ref=target.at[me],
                send_sem=send_sem.at[index], recv_sem=recv_sem.at[index],
                device_id={"expert": to_expert, "dp": to_dp}, device_id_type=MESH,
            ).start()

        every_peer(send)

    def wait(index, target, count):
        whole = target.at[pl.ds(0, count)]
        copy = pltpu.make_async_remote_copy(
            src_ref=whole, dst_ref=whole, send_sem=send_sem.at[index],
            recv_sem=recv_sem.at[index], device_id={"expert": expert, "dp": dp}, device_id_type=MESH,
        )
        copy.wait_recv()
        copy.wait_send()

    exchange(0, lambda to_expert, to_dp: send1.at[to_expert], recv1)
    wait(0, recv1, peers - 1)

    @pl.loop(0, peers // chunk)
    def _(index):
        block = recv1[pl.ds(index * chunk, chunk)].reshape(chunk * MSG, step)
        at = pl.ds(pl.multiple_of(index * lines, lines), lines)
        for q, (low, high) in enumerate(spans):
            piece = dot(of_chunk[q], block[:, : high - low], (1, 0)).astype(BF16)
            x_ref[at, low:high] = piece[:lines]
            g_ref[at, low:high] = piece[lines:]

    loads[3].wait()
    loads[4].wait()
    rows, g_rows = x_ref[...], g_ref[...]
    pre = dot(rows, inner_ref[...], (1, 0))
    g_hidden = dot(g_rows, outer_ref[...], (1, 1))
    scale = 0.7978845608028654
    tanh = jnp.tanh(scale * (pre + 0.044715 * (pre * pre * pre)))
    gate = 0.5 * (1.0 + tanh)
    hidden = (pre * gate).astype(BF16)
    slope = gate + (0.5 * pre) * (1.0 - tanh * tanh) * (scale * (1.0 + 0.134145 * (pre * pre)))
    g_pre = (g_hidden * slope).astype(BF16)
    hidden_ref[...] = hidden
    gpre_ref[...] = g_pre
    out_part = dot(hidden, outer_ref[...], (1, 0)).astype(BF16)
    g_part = dot(g_pre, inner_ref[...], (1, 1)).astype(BF16)
    for index in range(peers // chunk):
        at = slice(index * lines, (index + 1) * lines)
        both = jnp.concatenate([out_part[at], g_part[at]], axis=0)
        send2[index * chunk : (index + 1) * chunk] = pack(both, chunk, of_chunk).reshape(chunk, MSG, step)
    recv2[pl.ds(me, 1)] = send2[pl.ds(me, 1)]
    exchange(1, lambda to_expert, to_dp: send2.at[to_expert * dp_size + to_dp], recv2)
    shape = (2 * columns, peers * MSG)
    row = lax.broadcasted_iota(jnp.int32, shape, 0)
    line = lax.broadcasted_iota(jnp.int32, shape, 1)
    second = (row >= columns).astype(jnp.int32)
    column = row - second * columns
    per_expert = dp_size * MSG
    wanted = second * 2 + (column & 1)
    base = (column >> 1) * per_expert
    inside = (line >= base) & (line < base + per_expert)
    takes = [
        (inside & ((line & (MSG - 1)) == wanted + q * ROWS)).astype(BF16) for q in range(PIECES)
    ]
    wait(1, recv2, peers - 1)
    block = recv2[...].reshape(peers * MSG, step)

    sums = []
    for q, (low, high) in enumerate(spans):
        sums.append(dot(takes[q], block[:, : high - low], (1, 0)))
    total = jnp.concatenate(sums, axis=1)
    slot_out = total[:columns].astype(BF16)
    g_slot_in = total[columns:].astype(BF16)

    g_combine = dot(slot_out, cot_ref[...], (1, 1))
    g_logit = combine_exact * (
        g_combine - jnp.sum(combine_exact * g_combine, axis=0, keepdims=True)
    )
    g_dispatch = dot(g_slot_in, tokens, (1, 1))
    g_logit = g_logit + dispatch_exact * (
        g_dispatch - jnp.sum(dispatch_exact * g_dispatch, axis=1, keepdims=True)
    )
    g_logits = g_logit.astype(BF16)
    local = dot(g_logits, tokens, (1, 0))

    def fold(values):
        return jnp.concatenate([values[:, :half], values[:, half:]], axis=0).astype(BF16)

    def spread(index, target, own, axis, size):
        for offset in range(1, size):
            where = {"expert": expert, "dp": dp}
            where[axis] = shifted(own, offset, size)
            pltpu.make_async_remote_copy(
                src_ref=target.at[own], dst_ref=target.at[own], send_sem=send_sem.at[index],
                recv_sem=recv_sem.at[index], device_id=where, device_id_type=MESH,
            ).start()

    def add(target, size):
        folded = target[0].astype(F32)
        for index in range(1, size):
            folded = folded + target[index].astype(F32)
        return folded

    part_a[pl.ds(dp, 1)] = fold(local)[None]
    spread(2, part_a, dp, "dp", dp_size)
    left_ref[...] = jnp.concatenate([dispatch_exact, g_logits.astype(F32)], axis=0).astype(BF16)
    right_ref[:columns] = g_slot_in
    right_ref[columns:] = params_ref[...]
    wait(2, part_a, dp_size - 1)
    part_b[pl.ds(expert, 1)] = add(part_a, dp_size).astype(BF16)[None]
    spread(3, part_b, expert, "expert", experts)
    wait(3, part_b, experts - 1)
    folded = add(part_b, experts)
    gparams_ref[:, :half] = folded[:columns]
    gparams_ref[:, half:] = folded[columns:]


def weight_kernel(
    x_ref, g_ref, hidden_ref, gpre_ref, left_ref, right_ref, gparams_ref,
    gtok_hbm, gout_hbm, ginner_hbm, gouter_hbm, gtok_ref, ginner_ref, gouter_ref, store_sem,
):
    stores = []

    def product(left, right, out_ref, out_hbm):
        for low in range(0, out_ref.shape[0], 256):
            at = slice(low, min(low + 256, out_ref.shape[0]))
            out_ref[at] = dot(left[:, at], right[...], (0, 0)).astype(BF16)
            stores.append(pltpu.make_async_copy(
                out_ref.at[at], out_hbm.at[at], store_sem.at[len(stores)]
            ))
            stores[-1].start()

    product(x_ref, gpre_ref, ginner_ref, ginner_hbm)
    product(hidden_ref, g_ref, gouter_ref, gouter_hbm)
    product(left_ref, right_ref, gtok_ref, gtok_hbm)
    stores.append(pltpu.make_async_copy(gparams_ref, gout_hbm, store_sem.at[len(stores)]))
    stores[-1].start()
    for store in stores:
        store.wait()


def local(tokens, cotangent, slot_params, inner_weight, outer_weight):
    width = tokens.shape[2]
    patches = tokens.shape[1]
    columns = slot_params.shape[1]
    experts = lax.axis_size("expert")
    dp_size = lax.axis_size("dp")
    peers = experts * dp_size
    units = inner_weight.shape[2]
    rows = peers * 2
    step, _ = pieces_of(width)
    hbm = pl.BlockSpec(memory_space=pltpu.HBM)
    vmem = pl.BlockSpec(memory_space=pltpu.VMEM)
    shape = jax.ShapeDtypeStruct
    small = (
        shape((rows, width), BF16),
        shape((rows, width), BF16),
        shape((rows, units), BF16),
        shape((rows, units), BF16),
        shape((2 * columns, patches), BF16),
        shape((2 * columns, width), BF16),
        shape((columns, width), F32),
    )
    small = pl.pallas_call(
        functools.partial(kernel, experts, dp_size),
        out_shape=small,
        in_specs=[hbm] * 5,
        out_specs=[vmem] * 7,
        scratch_shapes=[
            pltpu.VMEM((patches, width), BF16),
            pltpu.VMEM((patches, width), BF16),
            pltpu.VMEM((columns, width), BF16),
            pltpu.VMEM((width, units), BF16),
            pltpu.VMEM((units, width), BF16),
            pltpu.VMEM((experts, MSG, step), BF16),
            pltpu.VMEM((peers, MSG, step), BF16),
            pltpu.VMEM((peers, MSG, step), BF16),
            pltpu.VMEM((peers, MSG, step), BF16),
            pltpu.VMEM((dp_size, 2 * columns, width // 2), BF16),
            pltpu.VMEM((experts, 2 * columns, width // 2), BF16),
            pltpu.SemaphoreType.DMA((5,)),
            pltpu.SemaphoreType.DMA((4,)),
            pltpu.SemaphoreType.DMA((4,)),
        ],
        compiler_params=pltpu.CompilerParams(
            collective_id=0, has_side_effects=True, vmem_limit_bytes=VMEM_BYTES
        ),
    )(tokens[0], cotangent[0], slot_params.T, inner_weight[0], outer_weight[0])
    results = (
        shape((patches, width), BF16),
        shape((columns, width), F32),
        shape((width, units), BF16),
        shape((units, width), BF16),
    )
    store_count = 1 + sum(-(-n // 256) for n in (patches, width, units))
    g_tokens, g_params, grad_inner, grad_outer = pl.pallas_call(
        weight_kernel,
        out_shape=results,
        in_specs=[vmem] * 7,
        out_specs=[hbm] * 4,
        scratch_shapes=[
            pltpu.VMEM((patches, width), BF16),
            pltpu.VMEM((width, units), BF16),
            pltpu.VMEM((units, width), BF16),
            pltpu.SemaphoreType.DMA((store_count,)),
        ],
        compiler_params=pltpu.CompilerParams(vmem_limit_bytes=VMEM_BYTES),
    )(*small)
    return g_tokens[None], g_params.T, grad_inner[None], grad_outer[None]


def solution(mesh):
    return jax.shard_map(
        local,
        mesh=mesh,
        in_specs=(
            P(("groups", "expert", "dp"), None, None),
            P(("groups", "expert", "dp"), None, None),
            P(),
            P("expert", None, "dp"),
            P("expert", "dp", None),
        ),
        out_specs=(
            P(("groups", "expert", "dp"), None, None),
            P("groups", None),
            P(("groups", "expert"), None, "dp"),
            P(("groups", "expert"), "dp", None),
        ),
        check_vma=False,
    )
```

```python
import functools

import jax
import jax.numpy as jnp
from jax import lax
from jax.experimental import pallas as pl
from jax.experimental.pallas import tpu as pltpu
from jax.sharding import PartitionSpec as P

F32, BF16 = jnp.float32, jnp.bfloat16
MESH = pl.DeviceIdType.MESH
ROWS, PIECES = 4, 4
MSG = ROWS * PIECES
CHUNK = 16
VMEM_BYTES = 54500 * 1024


def dot(a, b, contract, out=F32):
    return lax.dot_general(a, b, ((contract[:1], contract[1:]), ((), ())), preferred_element_type=out)


def pieces_of(width):
    step = -(-width // (PIECES * 128)) * 128
    return step, [(q * step, min(width, (q + 1) * step)) for q in range(PIECES)]


def select(messages):
    shape = (messages * ROWS, messages * MSG)
    row = lax.broadcasted_iota(jnp.int32, shape, 0)
    line = lax.broadcasted_iota(jnp.int32, shape, 1)
    half = (row >= messages * 2).astype(jnp.int32)
    inner = row - half * (messages * 2)
    shift = line - ((inner >> 1) * MSG + half * 2 + (inner & 1))
    return [(shift == q * ROWS).astype(BF16) for q in range(PIECES)]


def pack(rows, messages, chosen):
    width = rows.shape[1]
    step, spans = pieces_of(width)
    total = None
    for q, (low, high) in enumerate(spans):
        piece = rows[:, low:high]
        if high - low < step:
            piece = jnp.concatenate([piece, jnp.zeros((rows.shape[0], step - high + low), BF16)], axis=1)
        part = dot(chosen[q], piece, (0, 0))
        total = part if total is None else total + part
    return total.astype(BF16)


def kernel(
    experts, dp_size, tokens_hbm, cot_hbm, params_hbm, inner_hbm, outer_hbm,
    x_ref, g_ref, hidden_ref, gpre_ref, left_ref, right_ref, gparams_ref,
    tokens_ref, cot_ref, params_ref, inner_ref, outer_ref, send1, recv1, send2, recv2, part_a, part_b,
    load_sem, send_sem, recv_sem,
):
    peers = experts * dp_size
    expert = lax.axis_index("expert")
    dp = lax.axis_index("dp")
    me = expert * dp_size + dp
    width = tokens_ref.shape[1]
    step, spans = pieces_of(width)
    columns = params_ref.shape[0]
    half = width // 2

    pairs = (
        (params_hbm, params_ref), (tokens_hbm, tokens_ref), (cot_hbm, cot_ref),
        (inner_hbm, inner_ref), (outer_hbm, outer_ref),
    )
    loads = [pltpu.make_async_copy(a, b, load_sem.at[i]) for i, (a, b) in enumerate(pairs)]
    for load in loads:
        load.start()

    def shifted(own, offset, size):
        moved = own + offset
        return jnp.where(moved >= size, moved - size, moved)

    def every_peer(body):
        if peers <= CHUNK:
            for along in reversed(range(dp_size)):
                for across in reversed(range(experts)):
                    if across or along:
                        body(shifted(expert, across, experts), shifted(dp, along, dp_size))
        else:
            @pl.loop(1, peers)
            def _(offset):
                body(
                    shifted(expert, lax.div(offset, dp_size), experts),
                    shifted(dp, lax.rem(offset, dp_size), dp_size),
                )

    barrier = pltpu.get_barrier_semaphore()

    def greet(to_expert, to_dp):
        pl.semaphore_signal(
            barrier, inc=1, device_id={"expert": to_expert, "dp": to_dp}, device_id_type=MESH
        )

    every_peer(greet)
    chunk = min(CHUNK, peers)
    lines = chunk * 2
    of_experts, of_chunk = select(experts), select(chunk)

    loads[0].wait()
    loads[1].wait()
    tokens = tokens_ref[...]
    logits = dot(params_ref[...], tokens, (1, 1))
    e_t = jnp.exp(logits - jnp.max(logits, axis=1, keepdims=True))
    dispatch_exact = e_t / jnp.sum(e_t, axis=1, keepdims=True)
    e_c = jnp.exp(logits - jnp.max(logits, axis=0, keepdims=True))
    combine_exact = e_c / jnp.sum(e_c, axis=0, keepdims=True)
    dispatch = dispatch_exact.astype(BF16)
    slot_in = dot(dispatch, tokens, (1, 0))
    loads[2].wait()
    g_slot_out = dot(combine_exact.astype(BF16), cot_ref[...], (1, 0))
    both = jnp.concatenate([slot_in, g_slot_out], axis=0).astype(BF16)
    send1[...] = pack(both, experts, of_experts).reshape(experts, MSG, step)
    recv1[pl.ds(me, 1)] = send1[pl.ds(expert, 1)]

    pl.semaphore_wait(barrier, peers - 1)

    def exchange(index, source, target):
        def send(to_expert, to_dp):
            pltpu.make_async_remote_copy(
                src_ref=source(to_expert, to_dp), dst_ref=target.at[me],
                send_sem=send_sem.at[index], recv_sem=recv_sem.at[index],
                device_id={"expert": to_expert, "dp": to_dp}, device_id_type=MESH,
            ).start()

        every_peer(send)

    def wait(index, target, count):
        whole = target.at[pl.ds(0, count)]
        copy = pltpu.make_async_remote_copy(
            src_ref=whole, dst_ref=whole, send_sem=send_sem.at[index],
            recv_sem=recv_sem.at[index], device_id={"expert": expert, "dp": dp}, device_id_type=MESH,
        )
        copy.wait_recv()
        copy.wait_send()

    exchange(0, lambda to_expert, to_dp: send1.at[to_expert], recv1)
    wait(0, recv1, peers - 1)

    @pl.loop(0, peers // chunk)
    def _(index):
        block = recv1[pl.ds(index * chunk, chunk)].reshape(chunk * MSG, step)
        at = pl.ds(pl.multiple_of(index * lines, lines), lines)
        for q, (low, high) in enumerate(spans):
            piece = dot(of_chunk[q], block[:, : high - low], (1, 0)).astype(BF16)
            x_ref[at, low:high] = piece[:lines]
            g_ref[at, low:high] = piece[lines:]

    loads[3].wait()
    loads[4].wait()
    rows, g_rows = x_ref[...], g_ref[...]
    pre = dot(rows, inner_ref[...], (1, 0))
    g_hidden = dot(g_rows, outer_ref[...], (1, 1))
    scale = 0.7978845608028654
    tanh = jnp.tanh(scale * (pre + 0.044715 * (pre * pre * pre)))
    gate = 0.5 * (1.0 + tanh)
    hidden = (pre * gate).astype(BF16)
    slope = gate + (0.5 * pre) * (1.0 - tanh * tanh) * (scale * (1.0 + 0.134145 * (pre * pre)))
    g_pre = (g_hidden * slope).astype(BF16)
    hidden_ref[...] = hidden
    gpre_ref[...] = g_pre
    out_part = dot(hidden, outer_ref[...], (1, 0)).astype(BF16)
    g_part = dot(g_pre, inner_ref[...], (1, 1)).astype(BF16)
    for index in range(peers // chunk):
        at = slice(index * lines, (index + 1) * lines)
        both = jnp.concatenate([out_part[at], g_part[at]], axis=0)
        send2[index * chunk : (index + 1) * chunk] = pack(both, chunk, of_chunk).reshape(chunk, MSG, step)
    recv2[pl.ds(me, 1)] = send2[pl.ds(me, 1)]
    exchange(1, lambda to_expert, to_dp: send2.at[to_expert * dp_size + to_dp], recv2)
    shape = (2 * columns, peers * MSG)
    row = lax.broadcasted_iota(jnp.int32, shape, 0)
    line = lax.broadcasted_iota(jnp.int32, shape, 1)
    second = (row >= columns).astype(jnp.int32)
    column = row - second * columns
    per_expert = dp_size * MSG
    wanted = second * 2 + (column & 1)
    base = (column >> 1) * per_expert
    inside = (line >= base) & (line < base + per_expert)
    takes = [
        (inside & ((line & (MSG - 1)) == wanted + q * ROWS)).astype(BF16) for q in range(PIECES)
    ]
    wait(1, recv2, peers - 1)
    block = recv2[...].reshape(peers * MSG, step)

    sums = []
    for q, (low, high) in enumerate(spans):
        sums.append(dot(takes[q], block[:, : high - low], (1, 0)))
    total = jnp.concatenate(sums, axis=1)
    slot_out = total[:columns].astype(BF16)
    g_slot_in = total[columns:].astype(BF16)

    g_combine = dot(slot_out, cot_ref[...], (1, 1))
    g_logit = combine_exact * (
        g_combine - jnp.sum(combine_exact * g_combine, axis=0, keepdims=True)
    )
    g_dispatch = dot(g_slot_in, tokens, (1, 1))
    g_logit = g_logit + dispatch_exact * (
        g_dispatch - jnp.sum(dispatch_exact * g_dispatch, axis=1, keepdims=True)
    )
    g_logits = g_logit.astype(BF16)
    local = dot(g_logits, tokens, (1, 0))

    def fold(values):
        return jnp.concatenate([values[:, :half], values[:, half:]], axis=0).astype(BF16)

    def spread(index, target, own, axis, size):
        for offset in range(1, size):
            where = {"expert": expert, "dp": dp}
            where[axis] = shifted(own, offset, size)
            pltpu.make_async_remote_copy(
                src_ref=target.at[own], dst_ref=target.at[own], send_sem=send_sem.at[index],
                recv_sem=recv_sem.at[index], device_id=where, device_id_type=MESH,
            ).start()

    def add(target, size):
        folded = target[0].astype(F32)
        for index in range(1, size):
            folded = folded + target[index].astype(F32)
        return folded

    part_a[pl.ds(dp, 1)] = fold(local)[None]
    spread(2, part_a, dp, "dp", dp_size)
    left_ref[...] = jnp.concatenate([dispatch_exact, g_logits.astype(F32)], axis=0).astype(BF16)
    right_ref[:columns] = g_slot_in
    right_ref[columns:] = params_ref[...]
    wait(2, part_a, dp_size - 1)
    part_b[pl.ds(expert, 1)] = add(part_a, dp_size).astype(BF16)[None]
    spread(3, part_b, expert, "expert", experts)
    wait(3, part_b, experts - 1)
    folded = add(part_b, experts)
    gparams_ref[:, :half] = folded[:columns]
    gparams_ref[:, half:] = folded[columns:]


def weight_kernel(
    x_ref, g_ref, hidden_ref, gpre_ref, left_ref, right_ref, gparams_ref,
    gtok_hbm, gout_hbm, ginner_hbm, gouter_hbm, gtok_ref, ginner_ref, gouter_ref, store_sem,
):
    stores = []

    def product(left, right, out_ref, out_hbm):
        for low in range(0, out_ref.shape[0], 256):
            at = slice(low, min(low + 256, out_ref.shape[0]))
            out_ref[at] = dot(left[:, at], right[...], (0, 0)).astype(BF16)
            stores.append(pltpu.make_async_copy(
                out_ref.at[at], out_hbm.at[at], store_sem.at[len(stores)]
            ))
            stores[-1].start()

    product(x_ref, gpre_ref, ginner_ref, ginner_hbm)
    product(hidden_ref, g_ref, gouter_ref, gouter_hbm)
    product(left_ref, right_ref, gtok_ref, gtok_hbm)
    stores.append(pltpu.make_async_copy(gparams_ref, gout_hbm, store_sem.at[len(stores)]))
    stores[-1].start()
    for store in stores:
        store.wait()


def local(tokens, cotangent, slot_params, inner_weight, outer_weight):
    width = tokens.shape[2]
    patches = tokens.shape[1]
    columns = slot_params.shape[1]
    experts = lax.axis_size("expert")
    dp_size = lax.axis_size("dp")
    peers = experts * dp_size
    units = inner_weight.shape[2]
    rows = peers * 2
    step, _ = pieces_of(width)
    hbm = pl.BlockSpec(memory_space=pltpu.HBM)
    vmem = pl.BlockSpec(memory_space=pltpu.VMEM)
    shape = jax.ShapeDtypeStruct
    small = (
        shape((rows, width), BF16),
        shape((rows, width), BF16),
        shape((rows, units), BF16),
        shape((rows, units), BF16),
        shape((2 * columns, patches), BF16),
        shape((2 * columns, width), BF16),
        shape((columns, width), F32),
    )
    small = pl.pallas_call(
        functools.partial(kernel, experts, dp_size),
        out_shape=small,
        in_specs=[hbm] * 5,
        out_specs=[vmem] * 7,
        scratch_shapes=[
            pltpu.VMEM((patches, width), BF16),
            pltpu.VMEM((patches, width), BF16),
            pltpu.VMEM((columns, width), BF16),
            pltpu.VMEM((width, units), BF16),
            pltpu.VMEM((units, width), BF16),
            pltpu.VMEM((experts, MSG, step), BF16),
            pltpu.VMEM((peers, MSG, step), BF16),
            pltpu.VMEM((peers, MSG, step), BF16),
            pltpu.VMEM((peers, MSG, step), BF16),
            pltpu.VMEM((dp_size, 2 * columns, width // 2), BF16),
            pltpu.VMEM((experts, 2 * columns, width // 2), BF16),
            pltpu.SemaphoreType.DMA((5,)),
            pltpu.SemaphoreType.DMA((4,)),
            pltpu.SemaphoreType.DMA((4,)),
        ],
        compiler_params=pltpu.CompilerParams(
            collective_id=0, has_side_effects=True, vmem_limit_bytes=VMEM_BYTES
        ),
    )(tokens[0], cotangent[0], slot_params.T, inner_weight[0], outer_weight[0])
    results = (
        shape((patches, width), BF16),
        shape((columns, width), F32),
        shape((width, units), BF16),
        shape((units, width), BF16),
    )
    store_count = 1 + sum(-(-n // 256) for n in (patches, width, units))
    g_tokens, g_params, grad_inner, grad_outer = pl.pallas_call(
        weight_kernel,
        out_shape=results,
        in_specs=[vmem] * 7,
        out_specs=[hbm] * 4,
        scratch_shapes=[
            pltpu.VMEM((patches, width), BF16),
            pltpu.VMEM((width, units), BF16),
            pltpu.VMEM((units, width), BF16),
            pltpu.SemaphoreType.DMA((store_count,)),
        ],
        compiler_params=pltpu.CompilerParams(vmem_limit_bytes=VMEM_BYTES),
    )(*small)
    return g_tokens[None], g_params.T, grad_inner[None], grad_outer[None]


def solution(mesh):
    return jax.shard_map(
        local,
        mesh=mesh,
        in_specs=(
            P(("groups", "expert", "dp"), None, None),
            P(("groups", "expert", "dp"), None, None),
            P(),
            P("expert", None, "dp"),
            P("expert", "dp", None),
        ),
        out_specs=(
            P(("groups", "expert", "dp"), None, None),
            P("groups", None),
            P(("groups", "expert"), None, "dp"),
            P(("groups", "expert"), "dp", None),
        ),
        check_vma=False,
    )
```
